256 devices in a mesh: layer: 2 (over y_lo), row: 4 (over y_hi, core), col: 32 (over z, x).
Axes of the slice: x: 4, y: 4 (y_hi: 2, y_lo: 2; y = y_hi * 2 + y_lo), z: 8, core: 2. Of those that a mesh axis runs over, the one named last changes fastest.
Arguments:
- jac_values: bfloat16 [524288, 768], P(('layer', 'row', 'col')), may hold values from -0.046875 to 0.046875
- row_weights: bfloat16 [524288], P(('layer', 'row', 'col')), may hold values from 1 to 10
- block_cols: int32 [4096, 6], P(('layer', 'row', 'col')), may hold values from 0 to 127, as said below
Outputs:
- gain_band: float32 [16384, 1024], P(('layer', 'col'), 'row')
The draws below stay inside these ranges and needn't reach their ends.
Inputs may be any that keep to these rules, and one draw needn't show every extreme that they name: Row m of block_cols belongs to the device with linear index d = m // 16 in the order layer, row, col. With h = (d // 128) * 32 + d % 32, its 6 entries are distinct values ((2 * h + k) mod 128) with 0 <= k < 8.
All inputs are finite; a program needn't handle non-finite values.
Results may differ from the reference program's by a relative error of at most 0.0005.
Values sent between devices are 32-bit elements; how exact they have to be, the bound alone decides.
No kernel may reach another device: no remote copies, remote signals or barrier semaphores. Data moves between devices by JAX's collectives and lax.ppermute only.
A program may use at most 64 MiB of HBM per device.

```python
import math
from functools import partial
import jax
import jax.numpy as jnp
from jax import lax

BLOCK = 128
SLOTS = 6
SPAN = 8
BC_DEV = 2
BLK_DEV = 16
NB = 128
MB = 4096
N_ROW = 4
N_COL = 32


def draw_block_cols(key, part):
    key = jax.random.fold_in(key, 7)
    scores = jax.random.randint(key, (MB, SPAN), 0, 4096) * SPAN + jnp.arange(SPAN, dtype=jnp.int32)[None, :]
    ranking = jnp.argsort(scores, axis=1, stable=True).astype(jnp.int32)
    device = jnp.arange(MB, dtype=jnp.int32) // BLK_DEV
    home_index = device // (N_ROW * N_COL) * N_COL + device % N_COL
    return jnp.mod(BC_DEV * home_index[:, None] + ranking[:, :SLOTS], NB).astype(jnp.int32)


def block_levels(rng, dims, split, smallest, top_value):
    loudness = 1.0
    for dim, blocks in split:
        steps = jax.random.uniform(jax.random.fold_in(jax.random.fold_in(rng, 6), dim), (blocks,), jnp.float32, smallest / len(split), top_value / len(split))
        loudness = loudness * jnp.repeat(jnp.exp(steps), dims[dim] // blocks).reshape((-1,) + (1,) * (len(dims) - 1 - dim))
    return loudness


def gaussian(own_key, dims, scale, limit, split=(), kind=jnp.bfloat16):
    entries = jax.random.normal(own_key, dims, jnp.float32) * scale
    if len(split) > 0:
        entries = block_levels(own_key, dims, split, -0.22, 0.18) * entries
    return jnp.clip(entries, min=-limit, max=limit).astype(kind)


def setup_inputs(seed: int = 0) -> dict:
    keys = jax.random.split(jax.random.key(seed), 4)
    jac_values = gaussian(keys[0], (MB * BLOCK, SLOTS * BLOCK), (8 * BLK_DEV * BLOCK) ** -0.5, 0.046875, ((0, 256),))
    row_weights = jnp.clip(jnp.exp(math.log(10.0) - 2.3025851 * jax.random.uniform(keys[1], (MB * BLOCK,), jnp.float32) ** block_levels(keys[1], (MB * BLOCK,), ((0, 256),), -0.2, 0.2)), 1.0, 10.0).astype(jnp.bfloat16)
    block_cols = draw_block_cols(jax.random.fold_in(keys[3], 71), 0)
    return dict(jac_values=jac_values, row_weights=row_weights, block_cols=block_cols)


def band_matrix(values, slot_cols, first_block):
    blocks = slot_cols.shape[0]
    offsets = jnp.mod(slot_cols - first_block, NB).astype(jnp.int32)
    select = (offsets[:, :, None] == jnp.arange(SPAN, dtype=jnp.int32)[None, None, :]).astype(jnp.float32)
    pieces = values.astype(jnp.float32).reshape(blocks, BLOCK, SLOTS, BLOCK)
    banded = jnp.einsum("bmkc,bks->bmsc", pieces, select, precision=lax.Precision.HIGHEST)
    return banded.reshape(blocks * BLOCK, SPAN * BLOCK)


def home_product(jac_values, row_weights, block_cols, home_index):
    layer_of = home_index // N_COL
    col_of = home_index % N_COL
    first_block = (BC_DEV * home_index).astype(jnp.int32)
    summed = jnp.zeros((SPAN * BLOCK, SPAN * BLOCK), jnp.float32)
    for row_of in range(N_ROW):
        device = ((layer_of * N_ROW + row_of) * N_COL + col_of).astype(jnp.int32)
        start = (device * BLK_DEV * BLOCK).astype(jnp.int32)
        values = lax.dynamic_slice_in_dim(jac_values, start, BLK_DEV * BLOCK, 0)
        weights = lax.dynamic_slice_in_dim(row_weights, start, BLK_DEV * BLOCK, 0)
        slot_cols = lax.dynamic_slice_in_dim(block_cols, (device * BLK_DEV).astype(jnp.int32), BLK_DEV, 0)
        banded = band_matrix(values, slot_cols, first_block)
        weighted = (weights.astype(jnp.float32)[:, None] * banded).astype(jnp.bfloat16)
        summed = summed + jnp.dot(banded.T, weighted.astype(jnp.float32), precision=lax.Precision.HIGHEST)
    return summed


def reference(jac_values, row_weights, block_cols):
    home_total = NB // BC_DEV
    homes = jnp.arange(home_total, dtype=jnp.int32)
    products = lax.map(partial(home_product, jac_values, row_weights, block_cols), homes)
    products = products.reshape(home_total, SPAN, BLOCK, SPAN, BLOCK)
    rows_out = []
    for within in range(BC_DEV):
        cols_out = []
        for offset in range(SPAN):
            tile = jnp.zeros((home_total, BLOCK, BLOCK), jnp.float32)
            for distance in range(SPAN // BC_DEV):
                source = BC_DEV * distance + within
                target = source + offset
                if target < SPAN:
                    tile = tile + jnp.roll(products[:, source, :, target, :], distance, axis=0)
            cols_out.append(tile)
        rows_out.append(jnp.stack(cols_out, axis=2))
    gain = jnp.stack(rows_out, axis=1)
    return gain.reshape(NB * BLOCK, SPAN * BLOCK)
```

```python
import jax
import jax.numpy as jnp
from jax import lax
from jax.experimental import pallas as pl
from jax.experimental.pallas import tpu as pltpu
from jax.sharding import PartitionSpec as P

BLOCK = 128
SPAN = 8
SLOTS = 6
HOMES = 64
COLS = 32
WINDOW = 128
AXES = ("layer", "row", "col")

CORE_OFFSETS = ((0, 1, 4, 5), (2, 3, 6, 7))


def device_index(home, row):
    return ((home // COLS) * 4 + row) * COLS + home % COLS


def pairs_of(rows, distance):
    return [
        (device_index(home, source), device_index((home + distance) % HOMES, target))
        for source, target in rows
        for home in range(HOMES)
    ]


def slot_tiles(distance, core):
    tiles = []
    for offset in CORE_OFFSETS[core]:
        for within in range(2):
            source = 2 * distance + within
            tiles.append((source + offset, source) if source + offset < SPAN else None)
    return tiles


def store_tiles(product, first_target, distance, slots, base, core, out_ref):
    for owner in range(2):
        place = jnp.bitwise_xor(core, owner)
        tiles = slot_tiles(distance, owner)
        for slot in range(slots):
            if tiles[slot] is None:
                value = jnp.zeros((BLOCK, BLOCK), jnp.float32)
            else:
                target, source = tiles[slot]
                top = (target - first_target) * BLOCK
                left = (source - 2 * distance) * BLOCK
                value = product[top : top + BLOCK, left : left + BLOCK]
            out_ref[place, base + slot] = value


def transpose_block(h_ref, w_ref, at_ref, block, first, count):
    rows = pl.ds(block * BLOCK, BLOCK)
    weights = w_ref[pl.ds(block, 1), :].astype(jnp.float32)
    for target in range(count):
        tile = h_ref[rows, (first + target) * BLOCK : (first + target + 1) * BLOCK]
        turned = tile.T.astype(jnp.float32) * weights
        at_ref[target * BLOCK : (target + 1) * BLOCK, pl.ds(block * BLOCK, BLOCK)] = turned.astype(jnp.bfloat16)


def far_kernel(cols_ref, w_ref, jac_ref, h_ref, at_ref, out_ref, sems):
    home = lax.axis_index("layer") * COLS + lax.axis_index("col")
    core = lax.axis_index("row") % 2
    blocks = jac_ref.shape[0] // BLOCK

    def fetch(block, carry):
        rows = pl.ds(pl.multiple_of(block * BLOCK, BLOCK), BLOCK)
        h_ref[rows, :] = jnp.zeros((BLOCK, SPAN * BLOCK), jnp.bfloat16)
        for slot in range(SLOTS):
            offset = jnp.bitwise_and(cols_ref[slot, block] - 2 * home, WINDOW - 1)
            pltpu.make_async_copy(
                jac_ref.at[rows, slot * BLOCK : (slot + 1) * BLOCK],
                h_ref.at[rows, pl.ds(pl.multiple_of(offset * BLOCK, BLOCK), BLOCK)],
                sems.at[block],
            ).start()
        return carry

    lax.fori_loop(0, blocks, fetch, 0)

    for block in range(blocks):
        rows = pl.ds(block * BLOCK, BLOCK)
        pltpu.make_async_copy(
            jac_ref.at[rows, :], h_ref.at[rows, 0 : SLOTS * BLOCK], sems.at[block]
        ).wait()
        transpose_block(h_ref, w_ref, at_ref, block, 4, 4)

    product = jnp.dot(at_ref[...], h_ref[:, 512:768], preferred_element_type=jnp.float32)
    store_tiles(product, 4, 2, 4, 0, core, out_ref)
    product = jnp.dot(at_ref[256:, :], h_ref[:, 768:1024], preferred_element_type=jnp.float32)
    store_tiles(product, 6, 3, 3, 4, core, out_ref)


def middle_kernel(w_ref, h_ref, hi_ref, at_ref, out_ref):
    core = lax.axis_index("row") % 2
    for block in range(h_ref.shape[0] // BLOCK):
        transpose_block(h_ref, w_ref, at_ref, block, 2, 2)
    product = jnp.concatenate(
        [
            jnp.dot(at_ref[...], h_ref[:, 256:512], preferred_element_type=jnp.float32),
            jnp.dot(hi_ref[...], h_ref[:, 256:512], preferred_element_type=jnp.float32),
        ],
        axis=0,
    )
    store_tiles(product, 2, 1, 7, 0, core, out_ref)


def near_kernel(w_ref, h_ref, hi_ref, mid_ref, out_ref, at_ref):
    core = lax.axis_index("row") % 2
    for block in range(h_ref.shape[0] // BLOCK):
        transpose_block(h_ref, w_ref, at_ref, block, 0, 2)
    product = jnp.concatenate(
        [
            jnp.dot(at_ref[...], h_ref[:, 0:256], preferred_element_type=jnp.float32),
            jnp.dot(mid_ref[...], h_ref[:, 0:256], preferred_element_type=jnp.float32),
            jnp.dot(hi_ref[...], h_ref[:, 0:256], preferred_element_type=jnp.float32),
        ],
        axis=0,
    )
    store_tiles(product, 0, 0, 8, 0, core, out_ref)


def final_kernel(a_ref, b_ref, c_ref, d_ref, out_ref):
    for pair in range(2):
        for within in range(2):
            slot = 2 * pair + within
            tile = a_ref[slot] + b_ref[slot] + c_ref[slot] + d_ref[slot]
            out_ref[within * BLOCK : (within + 1) * BLOCK, pair * BLOCK : (pair + 1) * BLOCK] = tile.T


VMEM = pl.BlockSpec(memory_space=pltpu.VMEM)
SMEM = pl.BlockSpec(memory_space=pltpu.SMEM)
ANY = pl.BlockSpec(memory_space=pl.ANY)
PARAMS = pltpu.CompilerParams(vmem_limit_bytes=32 * 1024 * 1024)


def bf16(*shape):
    return jax.ShapeDtypeStruct(shape, jnp.bfloat16)


def f32(*shape):
    return jax.ShapeDtypeStruct(shape, jnp.float32)


def cost(rows, read, written):
    return pl.CostEstimate(flops=2 * rows * 256 * 2048, bytes_accessed=read + written, transcendentals=0)


def swap_core(value):
    return lax.ppermute(value, AXES, pairs_of([(0, 1), (1, 0), (2, 3), (3, 2)], 0))


def local(jac_values, row_weights, block_cols):
    rows = jac_values.shape[0]
    upper = lax.axis_index("row") >= 2
    weights = row_weights.reshape(rows // BLOCK, BLOCK)
    h, hi, far = pl.pallas_call(
        far_kernel,
        out_shape=(bf16(rows, 1024), bf16(512, rows), f32(2, 7, BLOCK, BLOCK)),
        in_specs=[SMEM, VMEM, ANY],
        out_specs=(VMEM, VMEM, VMEM),
        scratch_shapes=[pltpu.SemaphoreType.DMA((rows // BLOCK,))],
        compiler_params=PARAMS,
        cost_estimate=cost(768, 3 << 20, 0),
        name="far",
    )(block_cols.T, weights, jac_values)
    far_in = swap_core(far[1])
    mid, middle = pl.pallas_call(
        middle_kernel,
        out_shape=(bf16(256, rows), f32(2, 7, BLOCK, BLOCK)),
        in_specs=[VMEM] * 3,
        out_specs=(VMEM, VMEM),
        compiler_params=PARAMS,
        cost_estimate=cost(768, 0, 0),
        name="middle",
    )(weights, h, hi)
    far_sum = far[0] + far_in
    two = lax.ppermute(far_sum[:4], AXES, pairs_of([(r, r) for r in range(4)], 2))
    three = lax.ppermute(far_sum[4:], AXES, pairs_of([(0, 0), (2, 2)], 3))
    middle_in = swap_core(middle[1])
    near = pl.pallas_call(
        near_kernel,
        out_shape=f32(2, 8, BLOCK, BLOCK),
        in_specs=[VMEM] * 4,
        out_specs=VMEM,
        scratch_shapes=[pltpu.VMEM((256, rows), jnp.bfloat16)],
        compiler_params=PARAMS,
        cost_estimate=cost(1024, 0, 0),
        name="near",
    )(weights, h, hi, mid)
    middle_sum = middle[0] + middle_in
    low, high = middle_sum[:4], jnp.pad(middle_sum[4:], ((0, 1), (0, 0), (0, 0)))
    one_same = lax.ppermute(jnp.where(upper, high, low), AXES, pairs_of([(0, 0), (1, 1), (2, 2)], 1))
    one_cross = lax.ppermute(jnp.where(upper, low, high), AXES, pairs_of([(2, 0), (3, 1), (0, 2)], 1))
    near_in = swap_core(near[1])
    near_sum = near[0] + near_in
    low = near_sum[:4] + two + jnp.pad(three, ((0, 1), (0, 0), (0, 0)))
    high = near_sum[4:]
    crossed = lax.ppermute(jnp.where(upper, low, high), AXES, pairs_of([(0, 2), (1, 3), (2, 0), (3, 1)], 0))
    kept = jnp.where(upper, high, low)
    return pl.pallas_call(
        final_kernel,
        out_shape=f32(256, 256),
        in_specs=[VMEM] * 4,
        out_specs=VMEM,
        compiler_params=PARAMS,
        name="last",
    )(kept, crossed, one_same, one_cross)


def solution(mesh):
    in_specs = (P(AXES, None), P(AXES), P(AXES, None))
    return jax.shard_map(local, mesh=mesh, in_specs=in_specs, out_specs=P(("layer", "col"), "row"), check_vma=False)
```

```python
import jax
import jax.numpy as jnp
from jax import lax
from jax.experimental import pallas as pl
from jax.experimental.pallas import tpu as pltpu
from jax.sharding import PartitionSpec as P

BLOCK = 128
SPAN = 8
SLOTS = 6
HOMES = 64
COLS = 32
WINDOW = 128
AXES = ("layer", "row", "col")

def device_index(home, row):
    return ((home // COLS) * 4 + row) * COLS + home % COLS


def pairs_of(rows, distance):
    return [
        (device_index(home, source), device_index((home + distance) % HOMES, target))
        for source, target in rows
        for home in range(HOMES)
    ]


SMALL_PAIRS = pairs_of([(0, 0), (3, 1)], 3) + pairs_of([(1, 2), (2, 3)], 1)
ONE_PAIRS = pairs_of([(0, 0), (3, 1)], 1)
TWO_PAIRS = pairs_of([(1, 1), (2, 0)], 2)
CROSS_PAIRS = pairs_of([(2, 1), (1, 2)], 0)


def tile_at(distance, offset, within):
    source = 2 * distance + within
    return (distance, source, source + offset)


def tiles_of(distance, first_offset, count):
    tiles = [tile_at(distance, first_offset + slot // 2, slot % 2) for slot in range(count)]
    return [tile if tile[2] < SPAN else None for tile in tiles]


LEAD = 8
PAIR = "pair"


def with_pair(distance, count):
    return (distance, [PAIR] + tiles_of(distance, 1, count))


LARGE = (with_pair(1, 6), with_pair(2, 6))
SMALL = (with_pair(3, 1), (None, tiles_of(1, 4, 3)))
NEAR = (with_pair(0, 6), (None, tiles_of(0, 4, 7)))
LARGE_ROWS = LEAD + 7 * BLOCK
TWO_ROWS = LEAD + 6 * BLOCK
SMALL_ROWS = LEAD + 3 * BLOCK
HALF_ROWS = LEAD + 4 * BLOCK
SECOND_HALF = LEAD + 3 * BLOCK


def store_group(products, groups, base, count, first, keep_ref, send_ref):
    row_index = lax.broadcasted_iota(jnp.int32, (BLOCK, BLOCK), 0)
    col_index = lax.broadcasted_iota(jnp.int32, (BLOCK, BLOCK), 1)

    def plain(place):
        distance, source, target = place
        top = (target - 2 * distance) * BLOCK
        left = (source - 2 * distance) * BLOCK
        return products[distance][top : top + BLOCK, left : left + BLOCK]

    def lead_of(group):
        if group[0] is None:
            return jnp.zeros((LEAD, BLOCK), jnp.float32)
        tile = plain(tile_at(group[0], 0, 1))
        diagonal = jnp.sum(jnp.where(row_index == col_index, tile, 0.0), axis=0, keepdims=True)
        return jnp.broadcast_to(diagonal, (LEAD, BLOCK))

    def tile_of(group, slot):
        place = group[1][slot] if slot < len(group[1]) else None
        if place is None:
            return jnp.zeros((BLOCK, BLOCK), jnp.float32)
        if place == PAIR:
            return jnp.where(
                col_index >= row_index, plain(tile_at(group[0], 0, 0)), plain(tile_at(group[0], 0, 1))
            )
        return plain(place)

    def store(rows, zero, one):
        keep_ref[rows, :] = jnp.where(first, zero, one)
        send_ref[rows, :] = jnp.where(first, one, zero)

    store(slice(base, base + LEAD), lead_of(groups[0]), lead_of(groups[1]))
    for slot in range(count):
        top = base + LEAD + slot * BLOCK
        store(slice(top, top + BLOCK), tile_of(groups[0], slot), tile_of(groups[1], slot))


def far_kernel(cols_hbm, w_hbm, jac_ref, h_ref, at_ref, keep_ref, send_ref, stage, cols_ref, w_vmem, sems, side):
    home = lax.axis_index("layer") * COLS + lax.axis_index("col")
    row = lax.axis_index("row")
    first = (row == 0) | (row == 3)
    blocks = jac_ref.shape[0] // BLOCK
    parts = sems.shape[0]
    depth = blocks // parts * BLOCK
    cols_copy = pltpu.make_async_copy(cols_hbm, cols_ref, side.at[0])
    w_copy = pltpu.make_async_copy(w_hbm, w_vmem, side.at[1])
    cols_copy.start()
    w_copy.start()
    copies = []
    for part in range(parts):
        rows = slice(part * depth, (part + 1) * depth)
        copies.append(pltpu.make_async_copy(jac_ref.at[rows, :], stage.at[rows, :], sems.at[part]))
        copies[part].start()
    cols_copy.wait()
    w_copy.wait()
    weights = w_vmem[...].astype(jnp.float32)

    for block in range(blocks):
        if block * BLOCK % depth == 0:
            copies[block * BLOCK // depth].wait()
        rows = slice(block * BLOCK, (block + 1) * BLOCK)
        total, squares = jnp.int32(0), jnp.int32(0)
        for slot in range(SLOTS):
            offset = jnp.bitwise_and(cols_ref[slot, block] - 2 * home, WINDOW - 1)
            total, squares = total + offset, squares + offset * offset
            there = pl.ds(pl.multiple_of(offset * BLOCK, BLOCK), BLOCK)
            tile = stage[rows, slot * BLOCK : (slot + 1) * BLOCK]
            h_ref[rows, there] = tile
            turned = tile.T.astype(jnp.float32) * weights[block : block + 1, :]
            at_ref[there, rows] = turned.astype(jnp.bfloat16)
        total, squares = 28 - total, 140 - squares
        gap_square = 2 * squares - total * total
        gap = jnp.int32(0)
        for step in range(1, SPAN):
            gap = gap + jnp.where(gap_square >= step * step, 1, 0)
        for offset in ((total + gap) >> 1, (total - gap) >> 1):
            there = pl.ds(pl.multiple_of(offset * BLOCK, BLOCK), BLOCK)
            h_ref[rows, there] = jnp.zeros((BLOCK, BLOCK), jnp.bfloat16)
            at_ref[there, rows] = jnp.zeros((BLOCK, BLOCK), jnp.bfloat16)

    products = {
        distance: jnp.dot(
            at_ref[distance * 256 :, :],
            h_ref[:, distance * 256 : (distance + 1) * 256],
            preferred_element_type=jnp.float32,
        )
        for distance in (3, 2, 1)
    }
    store_group(products, LARGE, 0, 7, first, keep_ref, send_ref)
    store_group(products, SMALL, LARGE_ROWS, 3, first, keep_ref, send_ref)


def near_kernel(h_ref, at_ref, keep_ref, send_ref):
    product = jnp.dot(at_ref[...], h_ref[:, 0:256], preferred_element_type=jnp.float32)
    store_group({0: product}, NEAR, 0, 7, lax.axis_index("row") % 2 == 0, keep_ref, send_ref)


def final_kernel(a_ref, b_ref, out_ref, sum_ref):
    row = lax.axis_index("row")
    sum_ref[...] = a_ref[...] + b_ref[...]
    row_index = lax.broadcasted_iota(jnp.int32, (BLOCK, BLOCK), 0)
    col_index = lax.broadcasted_iota(jnp.int32, (BLOCK, BLOCK), 1)

    begin = jnp.where(row == 0, LEAD - BLOCK, jnp.where(row == 1, 0, jnp.where(row == 2, LEAD, BLOCK)))
    paired = sum_ref[LEAD : LEAD + BLOCK, :]
    turned = paired.T
    diagonal = jnp.broadcast_to(sum_ref[0:1, :], (BLOCK, BLOCK))
    symmetric = (
        jnp.where(col_index >= row_index, paired, turned),
        jnp.where(col_index < row_index, paired, jnp.where(col_index > row_index, turned, diagonal)),
    )
    for slot in range(4):
        place = begin + BLOCK * slot
        if slot == 0:
            place = jnp.maximum(place, 0)
        if slot == 3:
            place = jnp.where(row == 3, 0, place)
        tile = sum_ref[pl.ds(pl.multiple_of(place, 8), BLOCK), :].T
        if slot < 2:
            tile = jnp.where(row == 0, symmetric[slot], tile)
        if slot == 3:
            tile = jnp.where(row == 3, 0.0, tile)
        pair, within = slot // 2, slot % 2
        out_ref[within * BLOCK : (within + 1) * BLOCK, pair * BLOCK : (pair + 1) * BLOCK] = tile


VMEM = pl.BlockSpec(memory_space=pltpu.VMEM)
SMEM = pl.BlockSpec(memory_space=pltpu.SMEM)
HBM = pl.BlockSpec(memory_space=pltpu.HBM)
PARAMS = pltpu.CompilerParams(vmem_limit_bytes=16 * 1024 * 1024)


def bf16(*shape):
    return jax.ShapeDtypeStruct(shape, jnp.bfloat16)


def f32(*shape):
    return jax.ShapeDtypeStruct(shape, jnp.float32)


def cost(rows, read, written):
    return pl.CostEstimate(flops=2 * rows * 256 * 2048, bytes_accessed=read + written, transcendentals=0)


def swap_core(value):
    return lax.ppermute(value, AXES, pairs_of([(0, 1), (1, 0), (2, 3), (3, 2)], 0))


def local(jac_values, row_weights, block_cols):
    rows = jac_values.shape[0]
    row = lax.axis_index("row")
    first_core = row % 2 == 0
    owns = (row == 0) | (row == 3)
    far_rows = LARGE_ROWS + SMALL_ROWS
    inputs = (block_cols.T, row_weights.reshape(rows // BLOCK, BLOCK), jac_values)
    h, at, far, far_out = pl.pallas_call(
        far_kernel,
        out_shape=(bf16(rows, 1024), bf16(1024, rows), f32(far_rows, BLOCK), f32(far_rows, BLOCK)),
        in_specs=[HBM] * 3,
        out_specs=(VMEM,) * 4,
        scratch_shapes=[
            pltpu.VMEM(jac_values.shape, jnp.bfloat16),
            pltpu.SMEM((SLOTS, rows // BLOCK), jnp.int32),
            pltpu.VMEM((rows // BLOCK, BLOCK), jnp.bfloat16),
            pltpu.SemaphoreType.DMA((4,)),
            pltpu.SemaphoreType.DMA((2,)),
        ],
        compiler_params=PARAMS,
        cost_estimate=cost(1536, 3 << 20, 0),
        name="far",
    )(*(pltpu.with_memory_space_constraint(value, pltpu.HBM) for value in inputs))
    far_in = swap_core(far_out)
    near, near_out = pl.pallas_call(
        near_kernel,
        out_shape=(f32(LARGE_ROWS, BLOCK), f32(LARGE_ROWS, BLOCK)),
        in_specs=[VMEM] * 2,
        out_specs=(VMEM, VMEM),
        compiler_params=PARAMS,
        cost_estimate=cost(1024, 0, 0),
        name="near",
    )(h, at)
    near_in = swap_core(near_out)
    merged = near + near_in
    crossed = lax.ppermute(merged, AXES, CROSS_PAIRS)
    large = far[:LARGE_ROWS] + far_in[:LARGE_ROWS]
    one = lax.ppermute(large, AXES, ONE_PAIRS)
    two = lax.ppermute(large[:TWO_ROWS], AXES, TWO_PAIRS)
    small = lax.ppermute(far[LARGE_ROWS:] + far_in[LARGE_ROWS:], AXES, SMALL_PAIRS)
    total = jnp.where(owns, merged, 0.0) + one + crossed
    total = total + jnp.pad(two, ((0, LARGE_ROWS - TWO_ROWS), (0, 0)))
    total = total + jnp.pad(small, ((0, LARGE_ROWS - SMALL_ROWS), (0, 0)))
    low = total[:HALF_ROWS]
    high = jnp.pad(total[SECOND_HALF:], ((0, LEAD), (0, 0)))
    kept = jnp.where(first_core, low, high)
    other = swap_core(jnp.where(first_core, high, low))
    return pl.pallas_call(
        final_kernel,
        out_shape=f32(256, 256),
        in_specs=[VMEM] * 2,
        out_specs=VMEM,
        scratch_shapes=[pltpu.VMEM((HALF_ROWS, BLOCK), jnp.float32)],
        compiler_params=PARAMS,
        name="last",
    )(kept, other)


def solution(mesh):
    in_specs = (P(AXES, None), P(AXES), P(AXES, None))
    return jax.shard_map(local, mesh=mesh, in_specs=in_specs, out_specs=P(("layer", "col"), "row"), check_vma=False)
```

```python
import jax
import jax.numpy as jnp
from jax import lax
from jax.experimental import pallas as pl
from jax.experimental.pallas import tpu as pltpu
from jax.sharding import PartitionSpec as P

BLOCK = 128
SPAN = 8
SLOTS = 6
HOMES = 64
COLS = 32
WINDOW = 128
AXES = ("layer", "row", "col")

def device_index(home, row):
    return ((home // COLS) * 4 + row) * COLS + home % COLS


def pairs_of(rows, distance):
    return [
        (device_index(home, source), device_index((home + distance) % HOMES, target))
        for source, target in rows
        for home in range(HOMES)
    ]


SMALL_PAIRS = pairs_of([(0, 0), (3, 1)], 3) + pairs_of([(1, 2), (2, 3)], 1)
ONE_PAIRS = pairs_of([(0, 1), (3, 0)], 1)
TWO_PAIRS = pairs_of([(1, 0), (2, 1)], 2)
CROSS_PAIRS = pairs_of([(2, 1), (1, 2)], 0)


def tile_at(distance, offset, within):
    source = 2 * distance + within
    return (distance, source, source + offset)


def tiles_of(distance, first_offset, count):
    tiles = [tile_at(distance, first_offset + slot // 2, slot % 2) for slot in range(count)]
    return [tile if tile[2] < SPAN else None for tile in tiles]


LEAD = 8
PAIR = "pair"


def with_pair(distance, count):
    return (distance, [PAIR] + tiles_of(distance, 1, count))


LARGE = (with_pair(1, 6), with_pair(2, 6))
SMALL = (with_pair(3, 1), (None, tiles_of(1, 4, 3)))
NEAR = (with_pair(0, 6), (None, tiles_of(0, 4, 7)))
LARGE_ROWS = LEAD + 7 * BLOCK
TWO_ROWS = LEAD + 6 * BLOCK
SMALL_ROWS = LEAD + 3 * BLOCK
HALF_ROWS = LEAD + 4 * BLOCK
SECOND_HALF = LEAD + 3 * BLOCK


def store_group(products, groups, base, count, first, keep_ref, send_ref):
    row_index = lax.broadcasted_iota(jnp.int32, (BLOCK, BLOCK), 0)
    col_index = lax.broadcasted_iota(jnp.int32, (BLOCK, BLOCK), 1)

    def plain(place):
        distance, source, target = place
        top = (target - 2 * distance) * BLOCK
        left = (source - 2 * distance) * BLOCK
        return products[distance][top : top + BLOCK, left : left + BLOCK]

    def lead_of(group):
        if group[0] is None:
            return jnp.zeros((LEAD, BLOCK), jnp.float32)
        tile = plain(tile_at(group[0], 0, 1))
        diagonal = jnp.sum(jnp.where(row_index == col_index, tile, 0.0), axis=0, keepdims=True)
        return jnp.broadcast_to(diagonal, (LEAD, BLOCK))

    def tile_of(group, slot):
        place = group[1][slot] if slot < len(group[1]) else None
        if place is None:
            return jnp.zeros((BLOCK, BLOCK), jnp.float32)
        if place == PAIR:
            return jnp.where(
                col_index >= row_index, plain(tile_at(group[0], 0, 0)), plain(tile_at(group[0], 0, 1))
            )
        return plain(place)

    def store(rows, zero, one):
        keep_ref[rows, :] = jnp.where(first, zero, one)
        send_ref[rows, :] = jnp.where(first, one, zero)

    store(slice(base, base + LEAD), lead_of(groups[0]), lead_of(groups[1]))
    for slot in range(count):
        top = base + LEAD + slot * BLOCK
        store(slice(top, top + BLOCK), tile_of(groups[0], slot), tile_of(groups[1], slot))


def far_kernel(cols_hbm, w_hbm, jac_ref, h_ref, at_ref, keep_ref, send_ref, stage, cols_ref, w_vmem, sems, side):
    home = lax.axis_index("layer") * COLS + lax.axis_index("col")
    row = lax.axis_index("row")
    first = (row == 0) | (row == 3)
    blocks = jac_ref.shape[0] // BLOCK
    parts = sems.shape[0]
    depth = blocks // parts * BLOCK
    cols_copy = pltpu.make_async_copy(cols_hbm, cols_ref, side.at[0])
    w_copy = pltpu.make_async_copy(w_hbm, w_vmem, side.at[1])
    cols_copy.start()
    w_copy.start()
    copies = []
    for part in range(parts):
        rows = slice(part * depth, (part + 1) * depth)
        copies.append(pltpu.make_async_copy(jac_ref.at[rows, :], stage.at[rows, :], sems.at[part]))
        copies[part].start()
    h_ref[...] = jnp.zeros(h_ref.shape, jnp.bfloat16)
    at_ref[...] = jnp.zeros(at_ref.shape, jnp.bfloat16)
    cols_copy.wait()
    w_copy.wait()
    weights = w_vmem[...].astype(jnp.float32)

    for block in range(blocks):
        if block * BLOCK % depth == 0:
            copies[block * BLOCK // depth].wait()
        rows = slice(block * BLOCK, (block + 1) * BLOCK)
        for slot in range(SLOTS):
            offset = jnp.bitwise_and(cols_ref[slot, block] - 2 * home, WINDOW - 1)
            there = pl.ds(pl.multiple_of(offset * BLOCK, BLOCK), BLOCK)
            tile = stage[rows, slot * BLOCK : (slot + 1) * BLOCK]
            h_ref[rows, there] = tile
            turned = tile.T.astype(jnp.float32) * weights[block : block + 1, :]
            at_ref[there, rows] = turned.astype(jnp.bfloat16)

    products = {
        distance: jnp.dot(
            at_ref[distance * 256 :, :],
            h_ref[:, distance * 256 : (distance + 1) * 256],
            preferred_element_type=jnp.float32,
        )
        for distance in (3, 2, 1)
    }
    store_group(products, LARGE, 0, 7, first, keep_ref, send_ref)
    store_group(products, SMALL, LARGE_ROWS, 3, first, keep_ref, send_ref)


def near_kernel(h_ref, at_ref, keep_ref, send_ref):
    product = jnp.dot(at_ref[...], h_ref[:, 0:256], preferred_element_type=jnp.float32)
    store_group({0: product}, NEAR, 0, 7, lax.axis_index("row") % 2 == 0, keep_ref, send_ref)


def merge_kernel(a_ref, b_ref, large_ref, tiny_ref, out_ref):
    out_ref[...] = a_ref[...] + b_ref[...]


def final_kernel(a_ref, b_ref, out_ref, sum_ref):
    row = lax.axis_index("row")
    sum_ref[...] = a_ref[...] + b_ref[...]
    row_index = lax.broadcasted_iota(jnp.int32, (BLOCK, BLOCK), 0)
    col_index = lax.broadcasted_iota(jnp.int32, (BLOCK, BLOCK), 1)

    begin = jnp.where(row == 0, LEAD - BLOCK, jnp.where(row == 1, 0, jnp.where(row == 2, LEAD, BLOCK)))
    paired = sum_ref[LEAD : LEAD + BLOCK, :]
    turned = paired.T
    diagonal = jnp.broadcast_to(sum_ref[0:1, :], (BLOCK, BLOCK))
    symmetric = (
        jnp.where(col_index >= row_index, paired, turned),
        jnp.where(col_index < row_index, paired, jnp.where(col_index > row_index, turned, diagonal)),
    )
    for slot in range(4):
        place = begin + BLOCK * slot
        if slot == 0:
            place = jnp.maximum(place, 0)
        if slot == 3:
            place = jnp.where(row == 3, 0, place)
        tile = sum_ref[pl.ds(pl.multiple_of(place, 8), BLOCK), :].T
        if slot < 2:
            tile = jnp.where(row == 0, symmetric[slot], tile)
        if slot == 3:
            tile = jnp.where(row == 3, 0.0, tile)
        pair, within = slot // 2, slot % 2
        out_ref[within * BLOCK : (within + 1) * BLOCK, pair * BLOCK : (pair + 1) * BLOCK] = tile


VMEM = pl.BlockSpec(memory_space=pltpu.VMEM)
SMEM = pl.BlockSpec(memory_space=pltpu.SMEM)
HBM = pl.BlockSpec(memory_space=pltpu.HBM)
PARAMS = pltpu.CompilerParams(vmem_limit_bytes=16 * 1024 * 1024)


def bf16(*shape):
    return jax.ShapeDtypeStruct(shape, jnp.bfloat16)


def f32(*shape):
    return jax.ShapeDtypeStruct(shape, jnp.float32)


def cost(rows, read, written):
    return pl.CostEstimate(flops=2 * rows * 256 * 2048, bytes_accessed=read + written, transcendentals=0)


def swap_core(value):
    return lax.ppermute(value, AXES, pairs_of([(0, 1), (1, 0), (2, 3), (3, 2)], 0))


def local(jac_values, row_weights, block_cols):
    rows = jac_values.shape[0]
    row = lax.axis_index("row")
    first_core = row % 2 == 0
    owns = (row == 0) | (row == 3)
    far_rows = LARGE_ROWS + SMALL_ROWS
    inputs = (block_cols.T, row_weights.reshape(rows // BLOCK, BLOCK), jac_values)
    h, at, far, far_out = pl.pallas_call(
        far_kernel,
        out_shape=(bf16(rows, 1024), bf16(1024, rows), f32(far_rows, BLOCK), f32(far_rows, BLOCK)),
        in_specs=[HBM] * 3,
        out_specs=(VMEM,) * 4,
        scratch_shapes=[
            pltpu.VMEM(jac_values.shape, jnp.bfloat16),
            pltpu.SMEM((SLOTS, rows // BLOCK), jnp.int32),
            pltpu.VMEM((rows // BLOCK, BLOCK), jnp.bfloat16),
            pltpu.SemaphoreType.DMA((4,)),
            pltpu.SemaphoreType.DMA((2,)),
        ],
        compiler_params=PARAMS,
        cost_estimate=cost(1536, 3 << 20, 0),
        name="far",
    )(*(pltpu.with_memory_space_constraint(value, pltpu.HBM) for value in inputs))
    far_in = swap_core(far_out)
    near, near_out = pl.pallas_call(
        near_kernel,
        out_shape=(f32(LARGE_ROWS, BLOCK), f32(LARGE_ROWS, BLOCK)),
        in_specs=[VMEM] * 2,
        out_specs=(VMEM, VMEM),
        compiler_params=PARAMS,
        cost_estimate=cost(1024, 0, 0),
        name="near",
    )(h, at)
    near_in = swap_core(near_out)
    large = far[:LARGE_ROWS] + far_in[:LARGE_ROWS]
    tiny = far[LARGE_ROWS:] + far_in[LARGE_ROWS:]
    one = lax.ppermute(large, AXES, ONE_PAIRS)
    two = lax.ppermute(large[:TWO_ROWS], AXES, TWO_PAIRS)
    small = lax.ppermute(tiny, AXES, SMALL_PAIRS)
    merged = pl.pallas_call(
        merge_kernel,
        out_shape=f32(LARGE_ROWS, BLOCK),
        in_specs=[VMEM] * 2 + [pl.BlockSpec(memory_space=pl.ANY)] * 2,
        out_specs=VMEM,
        compiler_params=PARAMS,
        cost_estimate=pl.CostEstimate(flops=LARGE_ROWS * BLOCK, bytes_accessed=0, transcendentals=0),
        name="merge",
    )(near, near_in, large, tiny)
    crossed = lax.ppermute(merged, AXES, CROSS_PAIRS)
    total = jnp.where(owns, merged, 0.0) + one + crossed
    total = total + jnp.pad(two, ((0, LARGE_ROWS - TWO_ROWS), (0, 0)))
    total = total + jnp.pad(small, ((0, LARGE_ROWS - SMALL_ROWS), (0, 0)))
    low = total[:HALF_ROWS]
    high = jnp.pad(total[SECOND_HALF:], ((0, LEAD), (0, 0)))
    kept = jnp.where(first_core, low, high)
    other = swap_core(jnp.where(first_core, high, low))
    return pl.pallas_call(
        final_kernel,
        out_shape=f32(256, 256),
        in_specs=[VMEM] * 2,
        out_specs=VMEM,
        scratch_shapes=[pltpu.VMEM((HALF_ROWS, BLOCK), jnp.float32)],
        compiler_params=PARAMS,
        name="last",
    )(kept, other)


def solution(mesh):
    in_specs = (P(AXES, None), P(AXES), P(AXES, None))
    return jax.shard_map(local, mesh=mesh, in_specs=in_specs, out_specs=P(("layer", "col"), "row"), check_vma=False)
```

```python
import jax
import jax.numpy as jnp
from jax import lax
from jax.experimental import pallas as pl
from jax.experimental.pallas import tpu as pltpu
from jax.sharding import PartitionSpec as P

BLOCK = 128
SPAN = 8
SLOTS = 6
HOMES = 64
COLS = 32
WINDOW = 128
AXES = ("layer", "row", "col")

def device_index(home, row):
    return ((home // COLS) * 4 + row) * COLS + home % COLS


def pairs_of(rows, distance):
    return [
        (device_index(home, source), device_index((home + distance) % HOMES, target))
        for source, target in rows
        for home in range(HOMES)
    ]


SMALL_PAIRS = pairs_of([(0, 0), (3, 1)], 3) + pairs_of([(1, 3), (2, 2)], 1)
ONE_PAIRS = pairs_of([(0, 1), (3, 0)], 1)
TWO_PAIRS = pairs_of([(1, 0), (2, 1)], 2)
CROSS_PAIRS = pairs_of([(2, 1), (1, 2)], 0)


def tile_at(distance, offset, within):
    source = 2 * distance + within
    return (distance, source, source + offset)


def tiles_of(distance, first_offset, count):
    tiles = [tile_at(distance, first_offset + slot // 2, slot % 2) for slot in range(count)]
    return [tile if tile[2] < SPAN else None for tile in tiles]


LEAD = 8
PAIR = "pair"


def with_pair(distance, count):
    return (distance, [PAIR] + tiles_of(distance, 1, count))


LARGE = (with_pair(1, 6), with_pair(2, 6))
SMALL = (with_pair(3, 1), (None, tiles_of(1, 4, 3)))
NEAR = (with_pair(0, 6), (None, tiles_of(0, 4, 7)))
LARGE_ROWS = LEAD + 7 * BLOCK
TWO_ROWS = LEAD + 6 * BLOCK
SMALL_ROWS = LEAD + 3 * BLOCK
HALF_ROWS = LEAD + 4 * BLOCK
SECOND_HALF = LEAD + 3 * BLOCK


def store_group(products, groups, base, count, first, keep_ref, send_ref):
    row_index = lax.broadcasted_iota(jnp.int32, (BLOCK, BLOCK), 0)
    col_index = lax.broadcasted_iota(jnp.int32, (BLOCK, BLOCK), 1)

    def plain(place):
        distance, source, target = place
        top = (target - 2 * distance) * BLOCK
        left = (source - 2 * distance) * BLOCK
        return products[distance][top : top + BLOCK, left : left + BLOCK]

    def lead_of(group):
        if group[0] is None:
            return jnp.zeros((LEAD, BLOCK), jnp.float32)
        tile = plain(tile_at(group[0], 0, 1))
        diagonal = jnp.sum(jnp.where(row_index == col_index, tile, 0.0), axis=0, keepdims=True)
        return jnp.broadcast_to(diagonal, (LEAD, BLOCK))

    def tile_of(group, slot):
        place = group[1][slot] if slot < len(group[1]) else None
        if place is None:
            return jnp.zeros((BLOCK, BLOCK), jnp.float32)
        if place == PAIR:
            return jnp.where(
                col_index >= row_index, plain(tile_at(group[0], 0, 0)), plain(tile_at(group[0], 0, 1))
            )
        return plain(place)

    def store(rows, zero, one):
        keep_ref[rows, :] = jnp.where(first, zero, one)
        send_ref[rows, :] = jnp.where(first, one, zero)

    store(slice(base, base + LEAD), lead_of(groups[0]), lead_of(groups[1]))
    for slot in range(count):
        top = base + LEAD + slot * BLOCK
        store(slice(top, top + BLOCK), tile_of(groups[0], slot), tile_of(groups[1], slot))


def far_kernel(cols_hbm, w_hbm, jac_ref, h_ref, at_ref, keep_ref, send_ref, stage, cols_ref, w_vmem, sems, side):
    home = lax.axis_index("layer") * COLS + lax.axis_index("col")
    row = lax.axis_index("row")
    first = (row == 0) | (row == 3)
    blocks = jac_ref.shape[0] // BLOCK
    parts = sems.shape[0]
    depth = blocks // parts * BLOCK
    cols_copy = pltpu.make_async_copy(cols_hbm, cols_ref, side.at[0])
    w_copy = pltpu.make_async_copy(w_hbm, w_vmem, side.at[1])
    cols_copy.start()
    w_copy.start()
    copies = []
    for part in range(parts):
        rows = slice(part * depth, (part + 1) * depth)
        copies.append(pltpu.make_async_copy(jac_ref.at[rows, :], stage.at[rows, :], sems.at[part]))
        copies[part].start()
    h_ref[...] = jnp.zeros(h_ref.shape, jnp.bfloat16)
    at_ref[...] = jnp.zeros(at_ref.shape, jnp.bfloat16)
    cols_copy.wait()
    w_copy.wait()
    weights = w_vmem[...].astype(jnp.float32)

    for block in range(blocks):
        if block * BLOCK % depth == 0:
            copies[block * BLOCK // depth].wait()
        rows = slice(block * BLOCK, (block + 1) * BLOCK)
        for slot in range(SLOTS):
            offset = jnp.bitwise_and(cols_ref[slot, block] - 2 * home, WINDOW - 1)
            there = pl.ds(pl.multiple_of(offset * BLOCK, BLOCK), BLOCK)
            tile = stage[rows, slot * BLOCK : (slot + 1) * BLOCK]
            h_ref[rows, there] = tile
            turned = tile.T.astype(jnp.float32) * weights[block : block + 1, :]
            at_ref[there, rows] = turned.astype(jnp.bfloat16)

    products = {
        distance: jnp.dot(
            at_ref[distance * 256 :, :],
            h_ref[:, distance * 256 : (distance + 1) * 256],
            preferred_element_type=jnp.float32,
        )
        for distance in (3, 2, 1)
    }
    store_group(products, LARGE, 0, 7, first, keep_ref, send_ref)
    store_group(products, SMALL, LARGE_ROWS, 3, first, keep_ref, send_ref)


def near_kernel(h_ref, at_ref, keep_ref, send_ref):
    product = jnp.dot(at_ref[...], h_ref[:, 0:256], preferred_element_type=jnp.float32)
    store_group({0: product}, NEAR, 0, 7, lax.axis_index("row") % 2 == 0, keep_ref, send_ref)


def merge_kernel(a_ref, b_ref, large_ref, tiny_ref, out_ref):
    out_ref[...] = a_ref[...] + b_ref[...]


def final_kernel(a_ref, b_ref, out_ref, sum_ref):
    row = lax.axis_index("row")
    sum_ref[...] = a_ref[...] + b_ref[...]
    row_index = lax.broadcasted_iota(jnp.int32, (BLOCK, BLOCK), 0)
    col_index = lax.broadcasted_iota(jnp.int32, (BLOCK, BLOCK), 1)

    begin = jnp.where(row == 0, LEAD - BLOCK, jnp.where(row == 1, 0, jnp.where(row == 2, LEAD, BLOCK)))
    paired = sum_ref[LEAD : LEAD + BLOCK, :]
    turned = paired.T
    diagonal = jnp.broadcast_to(sum_ref[0:1, :], (BLOCK, BLOCK))
    symmetric = (
        jnp.where(col_index >= row_index, paired, turned),
        jnp.where(col_index < row_index, paired, jnp.where(col_index > row_index, turned, diagonal)),
    )
    for slot in range(4):
        place = begin + BLOCK * slot
        if slot == 0:
            place = jnp.maximum(place, 0)
        if slot == 3:
            place = jnp.where(row == 3, 0, place)
        tile = sum_ref[pl.ds(pl.multiple_of(place, 8), BLOCK), :].T
        if slot < 2:
            tile = jnp.where(row == 0, symmetric[slot], tile)
        if slot == 3:
            tile = jnp.where(row == 3, 0.0, tile)
        pair, within = slot // 2, slot % 2
        out_ref[within * BLOCK : (within + 1) * BLOCK, pair * BLOCK : (pair + 1) * BLOCK] = tile


VMEM = pl.BlockSpec(memory_space=pltpu.VMEM)
SMEM = pl.BlockSpec(memory_space=pltpu.SMEM)
HBM = pl.BlockSpec(memory_space=pltpu.HBM)
PARAMS = pltpu.CompilerParams(vmem_limit_bytes=16 * 1024 * 1024)


def bf16(*shape):
    return jax.ShapeDtypeStruct(shape, jnp.bfloat16)


def f32(*shape):
    return jax.ShapeDtypeStruct(shape, jnp.float32)


def cost(rows, read, written):
    return pl.CostEstimate(flops=2 * rows * 256 * 2048, bytes_accessed=read + written, transcendentals=0)


def swap_core(value):
    return lax.ppermute(value, AXES, pairs_of([(0, 1), (1, 0), (2, 3), (3, 2)], 0))


def local(jac_values, row_weights, block_cols):
    rows = jac_values.shape[0]
    row = lax.axis_index("row")
    first_core = row % 2 == 0
    owns = (row == 0) | (row == 3)
    far_rows = LARGE_ROWS + SMALL_ROWS
    inputs = (block_cols.T, row_weights.reshape(rows // BLOCK, BLOCK), jac_values)
    h, at, far, far_out = pl.pallas_call(
        far_kernel,
        out_shape=(bf16(rows, 1024), bf16(1024, rows), f32(far_rows, BLOCK), f32(far_rows, BLOCK)),
        in_specs=[HBM] * 3,
        out_specs=(VMEM,) * 4,
        scratch_shapes=[
            pltpu.VMEM(jac_values.shape, jnp.bfloat16),
            pltpu.SMEM((SLOTS, rows // BLOCK), jnp.int32),
            pltpu.VMEM((rows // BLOCK, BLOCK), jnp.bfloat16),
            pltpu.SemaphoreType.DMA((2,)),
            pltpu.SemaphoreType.DMA((2,)),
        ],
        compiler_params=PARAMS,
        cost_estimate=cost(1536, 3 << 20, 0),
        name="far",
    )(*(pltpu.with_memory_space_constraint(value, pltpu.HBM) for value in inputs))
    far_in = swap_core(far_out)
    near, near_out = pl.pallas_call(
        near_kernel,
        out_shape=(f32(LARGE_ROWS, BLOCK), f32(LARGE_ROWS, BLOCK)),
        in_specs=[VMEM] * 2,
        out_specs=(VMEM, VMEM),
        compiler_params=PARAMS,
        cost_estimate=cost(1024, 0, 0),
        name="near",
    )(h, at)
    near_in = swap_core(near_out)
    large = far[:LARGE_ROWS] + far_in[:LARGE_ROWS]
    tiny = far[LARGE_ROWS:] + far_in[LARGE_ROWS:]
    one = lax.ppermute(large, AXES, ONE_PAIRS)
    two = lax.ppermute(large[:TWO_ROWS], AXES, TWO_PAIRS)
    small = lax.ppermute(tiny, AXES, SMALL_PAIRS)
    merged = pl.pallas_call(
        merge_kernel,
        out_shape=f32(LARGE_ROWS, BLOCK),
        in_specs=[VMEM] * 2 + [pl.BlockSpec(memory_space=pl.ANY)] * 2,
        out_specs=VMEM,
        compiler_params=PARAMS,
        cost_estimate=pl.CostEstimate(flops=LARGE_ROWS * BLOCK, bytes_accessed=0, transcendentals=0),
        name="merge",
    )(near, near_in, large, tiny)
    crossed = lax.ppermute(merged, AXES, CROSS_PAIRS)
    total = jnp.where(owns, merged, 0.0) + one + crossed
    total = total + jnp.pad(two, ((0, LARGE_ROWS - TWO_ROWS), (0, 0)))
    total = total + jnp.pad(small, ((0, LARGE_ROWS - SMALL_ROWS), (0, 0)))
    low = total[:HALF_ROWS]
    high = jnp.pad(total[SECOND_HALF:], ((0, LEAD), (0, 0)))
    kept = jnp.where(first_core, low, high)
    other = swap_core(jnp.where(first_core, high, low))
    return pl.pallas_call(
        final_kernel,
        out_shape=f32(256, 256),
        in_specs=[VMEM] * 2,
        out_specs=VMEM,
        scratch_shapes=[pltpu.VMEM((HALF_ROWS, BLOCK), jnp.float32)],
        compiler_params=PARAMS,
        name="last",
    )(kept, other)


def solution(mesh):
    in_specs = (P(AXES, None), P(AXES), P(AXES, None))
    return jax.shard_map(local, mesh=mesh, in_specs=in_specs, out_specs=P(("layer", "col"), "row"), check_vma=False)
```

```python
import jax
import jax.numpy as jnp
from jax import lax
from jax.experimental import pallas as pl
from jax.experimental.pallas import tpu as pltpu
from jax.sharding import PartitionSpec as P

BLOCK = 128
SPAN = 8
SLOTS = 6
HOMES = 64
COLS = 32
WINDOW = 128
AXES = ("layer", "row", "col")

def device_index(home, row):
    return ((home // COLS) * 4 + row) * COLS + home % COLS


def pairs_of(rows, distance):
    return [
        (device_index(home, source), device_index((home + distance) % HOMES, target))
        for source, target in rows
        for home in range(HOMES)
    ]


SMALL_PAIRS = pairs_of([(0, 0), (3, 1)], 3) + pairs_of([(1, 3), (2, 2)], 1)
ONE_PAIRS = pairs_of([(0, 1), (3, 0)], 1)
TWO_PAIRS = pairs_of([(1, 0), (2, 1)], 2)
CROSS_PAIRS = pairs_of([(2, 1), (1, 2)], 0)


def tile_at(distance, offset, within):
    source = 2 * distance + within
    return (distance, source, source + offset)


def tiles_of(distance, first_offset, count):
    tiles = [tile_at(distance, first_offset + slot // 2, slot % 2) for slot in range(count)]
    return [tile if tile[2] < SPAN else None for tile in tiles]


LEAD = 8
PAIR = "pair"


def with_pair(distance, count):
    return (distance, [PAIR] + tiles_of(distance, 1, count))


LARGE = (with_pair(1, 6), with_pair(2, 6))
SMALL = (with_pair(3, 1), (None, tiles_of(1, 4, 3)))
NEAR = (with_pair(0, 6), (None, tiles_of(0, 4, 7)))
LARGE_ROWS = LEAD + 7 * BLOCK
TWO_ROWS = LEAD + 6 * BLOCK
SMALL_ROWS = LEAD + 3 * BLOCK
HALF_ROWS = LEAD + 4 * BLOCK
SECOND_HALF = LEAD + 3 * BLOCK


def store_group(products, groups, base, count, first, keep_ref, send_ref):
    row_index = lax.broadcasted_iota(jnp.int32, (BLOCK, BLOCK), 0)
    col_index = lax.broadcasted_iota(jnp.int32, (BLOCK, BLOCK), 1)

    def plain(place):
        distance, source, target = place
        top = (target - 2 * distance) * BLOCK
        left = (source - 2 * distance) * BLOCK
        return products[distance][top : top + BLOCK, left : left + BLOCK]

    def lead_of(group):
        if group[0] is None:
            return jnp.zeros((LEAD, BLOCK), jnp.float32)
        tile = plain(tile_at(group[0], 0, 1))
        diagonal = jnp.sum(jnp.where(row_index == col_index, tile, 0.0), axis=0, keepdims=True)
        return jnp.broadcast_to(diagonal, (LEAD, BLOCK))

    def tile_of(group, slot):
        place = group[1][slot] if slot < len(group[1]) else None
        if place is None:
            return jnp.zeros((BLOCK, BLOCK), jnp.float32)
        if place == PAIR:
            return jnp.where(
                col_index >= row_index, plain(tile_at(group[0], 0, 0)), plain(tile_at(group[0], 0, 1))
            )
        return plain(place)

    def store(rows, zero, one):
        keep_ref[rows, :] = jnp.where(first, zero, one)
        send_ref[rows, :] = jnp.where(first, one, zero)

    store(slice(base, base + LEAD), lead_of(groups[0]), lead_of(groups[1]))
    for slot in range(count):
        top = base + LEAD + slot * BLOCK
        store(slice(top, top + BLOCK), tile_of(groups[0], slot), tile_of(groups[1], slot))


def far_kernel(cols_hbm, w_hbm, jac_ref, h_ref, at_ref, keep_ref, send_ref, stage, cols_ref, w_vmem, sems, side):
    home = lax.axis_index("layer") * COLS + lax.axis_index("col")
    row = lax.axis_index("row")
    first = (row == 0) | (row == 3)
    blocks = jac_ref.shape[0] // BLOCK
    parts = sems.shape[0]
    depth = blocks // parts * BLOCK
    cols_copy = pltpu.make_async_copy(cols_hbm, cols_ref, side.at[0])
    w_copy = pltpu.make_async_copy(w_hbm, w_vmem, side.at[1])
    cols_copy.start()
    w_copy.start()
    copies = []
    for part in range(parts):
        rows = slice(part * depth, (part + 1) * depth)
        copies.append(pltpu.make_async_copy(jac_ref.at[rows, :], stage.at[rows, :], sems.at[part]))
        copies[part].start()
    h_ref[...] = jnp.zeros(h_ref.shape, jnp.bfloat16)
    at_ref[...] = jnp.zeros(at_ref.shape, jnp.bfloat16)
    cols_copy.wait()
    w_copy.wait()
    weights = w_vmem[...].astype(jnp.float32)

    for block in range(blocks):
        if block * BLOCK % depth == 0:
            copies[block * BLOCK // depth].wait()
        rows = slice(block * BLOCK, (block + 1) * BLOCK)
        for slot in range(SLOTS):
            offset = jnp.bitwise_and(cols_ref[slot, block] - 2 * home, WINDOW - 1)
            there = pl.ds(pl.multiple_of(offset * BLOCK, BLOCK), BLOCK)
            tile = stage[rows, slot * BLOCK : (slot + 1) * BLOCK]
            h_ref[rows, there] = tile
            turned = tile.T.astype(jnp.float32) * weights[block : block + 1, :]
            at_ref[there, rows] = turned.astype(jnp.bfloat16)

    products = {
        distance: jnp.dot(
            at_ref[distance * 256 :, :],
            h_ref[:, distance * 256 : (distance + 1) * 256],
            preferred_element_type=jnp.float32,
        )
        for distance in (3, 2, 1)
    }
    store_group(products, LARGE, 0, 7, first, keep_ref, send_ref)
    store_group(products, SMALL, LARGE_ROWS, 3, first, keep_ref, send_ref)


def near_kernel(h_ref, at_ref, keep_ref, send_ref):
    product = jnp.dot(at_ref[...], h_ref[:, 0:256], preferred_element_type=jnp.float32)
    store_group({0: product}, NEAR, 0, 7, lax.axis_index("row") % 2 == 0, keep_ref, send_ref)


def merge_kernel(a_ref, b_ref, out_ref):
    out_ref[...] = a_ref[...] + b_ref[...]


def final_kernel(a_ref, b_ref, out_ref, sum_ref):
    row = lax.axis_index("row")
    sum_ref[...] = a_ref[...] + b_ref[...]
    row_index = lax.broadcasted_iota(jnp.int32, (BLOCK, BLOCK), 0)
    col_index = lax.broadcasted_iota(jnp.int32, (BLOCK, BLOCK), 1)

    begin = jnp.where(row == 0, LEAD - BLOCK, jnp.where(row == 1, 0, jnp.where(row == 2, LEAD, BLOCK)))
    paired = sum_ref[LEAD : LEAD + BLOCK, :]
    turned = paired.T
    diagonal = jnp.broadcast_to(sum_ref[0:1, :], (BLOCK, BLOCK))
    symmetric = (
        jnp.where(col_index >= row_index, paired, turned),
        jnp.where(col_index < row_index, paired, jnp.where(col_index > row_index, turned, diagonal)),
    )
    for slot in range(4):
        place = begin + BLOCK * slot
        if slot == 0:
            place = jnp.maximum(place, 0)
        if slot == 3:
            place = jnp.where(row == 3, 0, place)
        tile = sum_ref[pl.ds(pl.multiple_of(place, 8), BLOCK), :].T
        if slot < 2:
            tile = jnp.where(row == 0, symmetric[slot], tile)
        if slot == 3:
            tile = jnp.where(row == 3, 0.0, tile)
        pair, within = slot // 2, slot % 2
        out_ref[within * BLOCK : (within + 1) * BLOCK, pair * BLOCK : (pair + 1) * BLOCK] = tile


VMEM = pl.BlockSpec(memory_space=pltpu.VMEM)
SMEM = pl.BlockSpec(memory_space=pltpu.SMEM)
HBM = pl.BlockSpec(memory_space=pltpu.HBM)
PARAMS = pltpu.CompilerParams(vmem_limit_bytes=16 * 1024 * 1024)


def bf16(*shape):
    return jax.ShapeDtypeStruct(shape, jnp.bfloat16)


def f32(*shape):
    return jax.ShapeDtypeStruct(shape, jnp.float32)


def cost(rows, read, written):
    return pl.CostEstimate(flops=2 * rows * 256 * 2048, bytes_accessed=read + written, transcendentals=0)


def swap_core(value):
    return lax.ppermute(value, AXES, pairs_of([(0, 1), (1, 0), (2, 3), (3, 2)], 0))


def local(jac_values, row_weights, block_cols):
    rows = jac_values.shape[0]
    row = lax.axis_index("row")
    first_core = row % 2 == 0
    owns = (row == 0) | (row == 3)
    far_rows = LARGE_ROWS + SMALL_ROWS
    inputs = (block_cols.T, row_weights.reshape(rows // BLOCK, BLOCK), jac_values)
    h, at, far, far_out = pl.pallas_call(
        far_kernel,
        out_shape=(bf16(rows, 1024), bf16(1024, rows), f32(far_rows, BLOCK), f32(far_rows, BLOCK)),
        in_specs=[HBM] * 3,
        out_specs=(VMEM,) * 4,
        scratch_shapes=[
            pltpu.VMEM(jac_values.shape, jnp.bfloat16),
            pltpu.SMEM((SLOTS, rows // BLOCK), jnp.int32),
            pltpu.VMEM((rows // BLOCK, BLOCK), jnp.bfloat16),
            pltpu.SemaphoreType.DMA((2,)),
            pltpu.SemaphoreType.DMA((2,)),
        ],
        compiler_params=PARAMS,
        cost_estimate=cost(1536, 3 << 20, 0),
        name="far",
    )(*(pltpu.with_memory_space_constraint(value, pltpu.HBM) for value in inputs))
    far_in = swap_core(far_out)
    near, near_out = pl.pallas_call(
        near_kernel,
        out_shape=(f32(LARGE_ROWS, BLOCK), f32(LARGE_ROWS, BLOCK)),
        in_specs=[VMEM] * 2,
        out_specs=(VMEM, VMEM),
        compiler_params=PARAMS,
        cost_estimate=cost(1024, 0, 0),
        name="near",
    )(h, at)
    near_in = swap_core(near_out)
    merged = pl.pallas_call(
        merge_kernel,
        out_shape=f32(LARGE_ROWS, BLOCK),
        in_specs=[VMEM] * 2,
        out_specs=VMEM,
        compiler_params=PARAMS,
        cost_estimate=pl.CostEstimate(flops=20000000000, bytes_accessed=0, transcendentals=0),
        name="merge",
    )(near, near_in)
    crossed = lax.ppermute(merged, AXES, CROSS_PAIRS)
    large = far[:LARGE_ROWS] + far_in[:LARGE_ROWS]
    one = lax.ppermute(large, AXES, ONE_PAIRS)
    two = lax.ppermute(large[:TWO_ROWS], AXES, TWO_PAIRS)
    small = lax.ppermute(far[LARGE_ROWS:] + far_in[LARGE_ROWS:], AXES, SMALL_PAIRS)
    total = jnp.where(owns, merged, 0.0) + one + crossed
    total = total + jnp.pad(two, ((0, LARGE_ROWS - TWO_ROWS), (0, 0)))
    total = total + jnp.pad(small, ((0, LARGE_ROWS - SMALL_ROWS), (0, 0)))
    low = total[:HALF_ROWS]
    high = jnp.pad(total[SECOND_HALF:], ((0, LEAD), (0, 0)))
    kept = jnp.where(first_core, low, high)
    other = swap_core(jnp.where(first_core, high, low))
    return pl.pallas_call(
        final_kernel,
        out_shape=f32(256, 256),
        in_specs=[VMEM] * 2,
        out_specs=VMEM,
        scratch_shapes=[pltpu.VMEM((HALF_ROWS, BLOCK), jnp.float32)],
        compiler_params=PARAMS,
        name="last",
    )(kept, other)


def solution(mesh):
    in_specs = (P(AXES, None), P(AXES), P(AXES, None))
    return jax.shard_map(local, mesh=mesh, in_specs=in_specs, out_specs=P(("layer", "col"), "row"), check_vma=False)
```
